32 devices in a mesh: groups: 2 (over x), dp: 8 (over z, y), expert: 2 (over core).
Axes of the slice: x: 2, y: 2, z: 4, core: 2. Of those that a mesh axis runs over, the one named last changes fastest.
Arguments:
- tokens: bfloat16 [4096, 6144], P(('groups', 'dp', 'expert')), parts along dimension 0, may hold values from -6 to 6
- out_grads: bfloat16 [4096, 2, 6144], P(('groups', 'dp', 'expert')), parts along dimension 0, may hold values from -6 to 6
- expert_ids: int32 [4096, 2], P(('groups', 'dp', 'expert')), parts along dimension 0, may hold values from 0 to 3, all different within a row; in each aligned block of 128 rows (0 to 127, 128 to 255, ...) at most 96 rows name the same one
Outputs:
- act_factor: float32 [64, 4, 6144], P(('groups', 'dp'), 'expert'), parts along dimension 0
- grad_factor: float32 [64, 4, 6144], P(('groups', 'dp'), 'expert'), parts along dimension 0
The draws below stay inside these ranges and needn't reach their ends.
There are 2 independent parts, one for each index of `groups`. The reference program is written for one: setup_inputs(seed, part) draws one part's arguments, and reference() takes and returns one part's arrays. A program takes and returns all parts, laid end to end along the dimension named above; each array names one. Nothing has to cross between parts.
Inputs may be any that keep to these rules, and one draw needn't show every extreme that they name: `expert_ids`: each row names 2 different experts. In the 128 rows of one device no expert is named by more than 96 rows, a bound that some block reaches of them.
All inputs are finite; a program needn't handle non-finite values.
Results may differ from the reference program's by a relative error of at most 0.0003.
Values may be sent and summed in bfloat16 or wider, within the bound.
A program may use at most 128 MiB of HBM per device.

```python
import math
import jax
import jax.numpy as jnp
import numpy as np
from jax import lax

D = 6144
TOP = 2
TOK_DEV = 128
EXPERTS = 4
TOKENS = 2048
CAP = 96
SLAB = 32


def with_spikes(drawn, stream_key, source, target, shards_of, factor):
    def block_of(axis_at):
        return (jnp.arange(drawn.shape[axis_at]) // (drawn.shape[axis_at] // shards_of)).reshape((-1,) + (1,) * (drawn.ndim - 1 - axis_at))

    near = jax.random.permutation(stream_key, shards_of)[block_of(target)]
    far = (block_of(target) + shards_of // 2) % shards_of
    return jnp.where((block_of(source) == near) | (block_of(source) == far), factor * drawn, drawn)


def steps_of(stream_key, shape, shards, smallest, high):
    def one(axis_at, blocks):
        draws = jax.random.uniform(jax.random.fold_in(jax.random.fold_in(stream_key, 6), axis_at), (blocks,), jnp.float32, smallest / len(shards), high / len(shards))
        return jnp.repeat(jnp.exp(draws), shape[axis_at] // blocks).reshape((-1,) + (1,) * (len(shape) - axis_at - 1))

    level = one(*shards[0])
    for cut in shards[1:]:
        level = level * one(*cut)
    return level


def assign_block(rng, own, number, rows, count, top, most, slope):
    ranking = jax.random.permutation(rng, count)
    crowded, usual = load_shares(count, rows * top, most, slope, True), load_shares(count, rows * top, most, slope, False)
    places = jnp.arange(count)

    def named(sizes, rotation):
        used = int((sizes > 0).sum())
        fixed = max(1, used // 4)
        moved = fixed + (places - fixed + rotation * (used - fixed)) % max(1, count - fixed)
        return jnp.zeros((count,), jnp.int32).at[ranking[jnp.where(places < fixed, places, moved)]].set(jnp.asarray(sizes, jnp.int32))

    sizes = jnp.where(number % 4 == 0, named(crowded, number // 4), named(usual, number - number // 4 - 1))
    mixed = jax.random.permutation(jax.random.fold_in(own, 3), count)
    giver, taker = mixed[0:count // 2 * 2:2], mixed[1:count // 2 * 2:2]
    margin = jnp.minimum(sizes[giver] - 1, most - sizes[taker]) // 2
    margin = jnp.where((giver == ranking[0]) | (taker == ranking[0]) | (sizes[taker] == 0), 0, jnp.maximum(margin, 0))
    moved = jax.random.randint(jax.random.fold_in(own, 4), (count // 2,), 0, 1 << 20) % (margin + 1)
    sizes = sizes.at[giver].add(-moved).at[taker].add(moved)
    members = jnp.searchsorted(jnp.cumsum(sizes), jnp.arange(rows * top), side="right").astype(jnp.int32)
    table = members.reshape(top, rows).T
    table = table[jax.random.permutation(jax.random.fold_in(own, 1), rows)]
    rotation = jax.random.randint(jax.random.fold_in(own, 2), (rows, 1), 0, top)
    return jnp.take_along_axis(table, (jnp.arange(top)[None, :] + rotation) % top, axis=1)


def load_shares(number_of, total, reach, skew, full):
    weights = [(1 << 20) // math.isqrt(rank ** skew) + 1 for rank in range(1, number_of + 1)]
    largest = reach if full else min(reach, max(-(-total // number_of), total * weights[0] // sum(weights)))
    least = 1 if total - largest >= number_of - 1 else 0
    counts, spare = [largest] + [least] * (number_of - 1), total - largest - least * (number_of - 1)
    while spare > 0:
        movable = [i for i in range(1, number_of) if counts[i] < largest] or [i for i in range(1, number_of) if counts[i] < reach]
        whole, remaining = sum([weights[i] for i in movable]), spare
        for i in movable:
            extra = min(reach - counts[i], max(1, remaining * weights[i] // whole), spare)
            counts[i] = counts[i] + extra
            spare = spare - extra
    return np.array(counts)


def noise_with(key, extent, spread, limit, shards, heavy, kind=jnp.bfloat16):
    values = spread * jax.random.normal(key, extent, jnp.float32)
    if shards:
        values = values * steps_of(key, extent, shards, -0.22, 0.18)
    return jnp.clip(with_spikes(values, jax.random.fold_in(key, 3), *heavy), -limit, limit).astype(kind)


def setup_inputs(seed: int = 0, part: int = 0) -> dict:
    streams_of = jax.random.split(jax.random.key(seed), 4)
    part_keys = jax.random.split(jax.random.fold_in(streams_of[3], part), 4)
    tokens = noise_with(part_keys[0], (TOKENS, D), 1.0, 6.0, ((0, 16),), (0, 1, 16, 2.0))
    out_grads = noise_with(part_keys[1], (TOKENS, TOP, D), 1.0, 6.0, ((0, 16),), (0, 2, 16, 2.0))
    expert_ids_keys = jax.random.split(jax.random.fold_in(part_keys[2], 1), TOKENS // TOK_DEV)
    expert_ids_turns = jax.random.permutation(jax.random.fold_in(part_keys[2], 3), TOKENS // TOK_DEV)
    expert_ids = jax.vmap(lambda own, number: assign_block(jax.random.fold_in(part_keys[2], 2), own, number, TOK_DEV, EXPERTS, TOP, CAP, 2))(expert_ids_keys, expert_ids_turns).reshape((TOKENS, TOP))
    return {"tokens": tokens, "out_grads": out_grads, "expert_ids": expert_ids}


def expert_grams(inputs, grads, expert_ids, index):
    hit = expert_ids == index
    chosen = jnp.any(hit, axis=1)
    masked_in = jnp.where(chosen[:, None], inputs, jnp.zeros_like(inputs))
    act = jnp.dot(masked_in[:, :SLAB].T, inputs, precision=lax.Precision.HIGHEST)
    picked = jnp.sum(jnp.where(hit[:, :, None], grads, jnp.zeros_like(grads)), axis=1)
    grad = jnp.dot(picked[:, :SLAB].T, picked, precision=lax.Precision.HIGHEST)
    return act / TOKENS, grad / TOKENS


def reference(tokens, out_grads, expert_ids):
    inputs = tokens.astype(jnp.float32)
    grads = out_grads.astype(jnp.float32)
    indices = jnp.arange(EXPERTS, dtype=jnp.int32)
    act_all, grad_all = lax.map(lambda index: expert_grams(inputs, grads, expert_ids, index), indices)
    return jnp.transpose(act_all, (1, 0, 2)), jnp.transpose(grad_all, (1, 0, 2))
```

```python
import functools

import jax
import jax.numpy as jnp
from jax import lax
from jax.experimental import pallas as pl
from jax.experimental.pallas import tpu as pltpu
from jax.sharding import PartitionSpec as P

EXP_DEV = 2
ROWS_DEV = 4
BLK = EXP_DEV * ROWS_DEV
PAIR = 2 * BLK
LANES = 128
WIDTH = 768
STEPS = 8.0
FULL = 32760.0
TINY = 1e-37
LAG_Y, LAG_Z, LAG_OUT = 1, 3, 4


def encode(tiles, dst):
    top = functools.reduce(jnp.maximum, [jnp.abs(t) for t in tiles])
    step = jnp.ceil(jnp.log2(jnp.maximum(top, TINY)) * STEPS)
    scale = jnp.exp2(step * (-1.0 / STEPS)) * FULL
    for j, t in enumerate(tiles):
        dst(j, jnp.round(t * scale).astype(jnp.int32).astype(jnp.int16))
    dst(len(tiles), step.astype(jnp.int32).astype(jnp.int16))


def widen(x):
    return x.astype(jnp.int32).astype(jnp.float32)


def unit_of(codes):
    return jnp.exp2(widen(codes) * (1.0 / STEPS)) * (1.0 / FULL)


def kernel(
    n, width, total,
    ids_ref, tok_ref, grad_ref, act_ref, gout_ref,
    x_buf, g_buf, part, r0, s1, r1, s2, r2,
    in_sem, s0_sem, r0_sem, s1_sem, r1_sem, s2_sem, r2_sem,
):
    tok_rows, features = tok_ref.shape
    items = features // width
    tiles = width // LANES
    nz = n // 2
    half = n * PAIR
    quarter = half // 2
    core = lax.axis_index("expert")
    d = lax.axis_index("dp")
    z, y = d // 2, lax.rem(d, 2)

    flat = grad_ref.reshape(2 * tok_rows, features)
    loads = []
    for i in range(items):
        cols = pl.ds(i * width, width)
        pair = (
            pltpu.make_async_copy(tok_ref.at[:, cols], x_buf.at[i], in_sem.at[0, i]),
            pltpu.make_async_copy(flat.at[:, cols], g_buf.at[i], in_sem.at[1, i]),
        )
        for c in pair:
            c.start()
        loads.append(pair)

    sibling = {"expert": 1 - core}
    across = {"dp": z * 2 + 1 - y}
    peers = [{"dp": lax.rem(z + 1 + j, nz) * 2 + y} for j in range(nz - 1)]
    barrier = pltpu.get_barrier_semaphore()
    for dev in [sibling, across] + peers:
        pl.semaphore_signal(barrier, inc=1, device_id=dev, device_id_type=pl.DeviceIdType.MESH)

    m_rows = 2 * n * BLK
    slab = -(-ROWS_DEV * n // LANES) * LANES

    def row_of(m):
        zd = z + 1 + (m & (n * BLK // 2 - 1)) // BLK
        zd = jnp.where(zd >= nz, zd - nz, zd)
        yd = (y + 1 + (m & (n * BLK - 1)) // (n * BLK // 2)) & 1
        return ROWS_DEV * (2 * zd + yd) + (m & (BLK - 1)) // EXP_DEV

    def expert_of(m):
        return EXP_DEV * ((core + 1 + m // (n * BLK)) & 1) + (m & (EXP_DEV - 1))

    pick = (
        row_of(lax.broadcasted_iota(jnp.int32, (m_rows, slab), 0))
        == lax.broadcasted_iota(jnp.int32, (m_rows, slab), 1)
    ).astype(jnp.float32).astype(jnp.bfloat16)
    ids = ids_ref[...]
    spread = (
        lax.broadcasted_iota(jnp.int32, (tok_rows, 2 * tok_rows), 1) // 2
        == lax.broadcasted_iota(jnp.int32, (tok_rows, 2 * tok_rows), 0)
    ).astype(jnp.float32).astype(jnp.bfloat16)
    ids_f = ids.astype(jnp.float32)
    both = jnp.dot(ids_f.astype(jnp.bfloat16), spread, preferred_element_type=jnp.float32)
    odd = (lax.broadcasted_iota(jnp.int32, (1, 2 * tok_rows), 1) & 1) == 1
    ids_flat = jnp.where(odd, both[1:2, :], both[0:1, :])
    e_tok = expert_of(lax.broadcasted_iota(jnp.int32, (m_rows, tok_rows), 0)).astype(jnp.float32)
    e_pair = expert_of(lax.broadcasted_iota(jnp.int32, (m_rows, 2 * tok_rows), 0)).astype(
        jnp.float32
    )
    nt = (((1,), (1,)), ((), ()))

    for c in loads[0]:
        c.wait()
    left_x = lax.dot_general(pick, x_buf[0, :, :slab], nt, preferred_element_type=jnp.float32)
    left_g = lax.dot_general(pick, g_buf[0, :, :slab], nt, preferred_element_type=jnp.float32)
    hit_x = (e_tok == ids_f[0:1, :]) | (e_tok == ids_f[1:2, :])
    left_x = jnp.where(hit_x, left_x, 0.0).astype(jnp.bfloat16)
    left_g = jnp.where(e_pair == ids_flat, left_g, 0.0).astype(jnp.bfloat16)

    pl.semaphore_wait(barrier, nz + 1)

    def send(src, dst, s_sem, r_sem, dev):
        return pltpu.make_async_remote_copy(
            src_ref=src, dst_ref=dst, send_sem=s_sem, recv_sem=r_sem,
            device_id=dev, device_id_type=pl.DeviceIdType.MESH,
        )

    core_copy = [
        send(part.at[i, pl.ds(0, half)], r0.at[i], s0_sem.at[i], r0_sem.at[i], sibling)
        for i in range(items)
    ]
    y_copy = [
        send(s1.at[i], r1.at[i], s1_sem.at[i], r1_sem.at[i], across) for i in range(items)
    ]
    z_copy = [
        [
            send(s2.at[i, j], r2.at[i, j], s2_sem.at[i, j], r2_sem.at[i, j], peers[j])
            for j in range(nz - 1)
        ]
        for i in range(items)
    ]

    def local_terms(i):
        if i:
            for c in loads[i]:
                c.wait()
        for a, (left, buf) in enumerate(((left_x, x_buf), (left_g, g_buf))):
            term = jnp.dot(left, buf[i], preferred_element_type=jnp.float32)
            for b in range(m_rows // BLK):
                part[i, b * PAIR + a * BLK : b * PAIR + (a + 1) * BLK, :] = term[
                    b * BLK : (b + 1) * BLK
                ]
        core_copy[i].start()

    def lane(j):
        return slice(j * LANES, (j + 1) * LANES)

    def chip_terms(i):
        core_copy[i].wait_recv()
        for b in range(quarter // PAIR):
            rows = slice(b * PAIR, (b + 1) * PAIR)
            own = slice(half + b * PAIR, half + (b + 1) * PAIR)
            sums = [part[i, own, lane(j)] + r0[i, rows, lane(j)] for j in range(tiles)]

            def put(j, v):
                s1[i, rows, lane(j)] = v

            encode(sums, put)
        y_copy[i].start()

    def pair_terms(i):
        y_copy[i].wait_recv()
        for b in range(nz):
            rows = slice(b * PAIR, (b + 1) * PAIR)
            near = slice(quarter + b * PAIR, quarter + (b + 1) * PAIR)
            own = slice(half + quarter + b * PAIR, half + quarter + (b + 1) * PAIR)
            unit = unit_of(r1[i, rows, lane(tiles)])
            sums = [
                part[i, own, lane(j)]
                + r0[i, near, lane(j)]
                + widen(r1[i, rows, lane(j)]) * unit
                for j in range(tiles)
            ]
            if b < nz - 1:

                def put(j, v):
                    s2[i, b, :, lane(j)] = v

                encode(sums, put)
                z_copy[i][b].start()
            else:
                for j in range(tiles):
                    part[i, own, lane(j)] = sums[j]

    def outputs(i):
        for c in z_copy[i]:
            c.wait_recv()
        last = slice(2 * half - PAIR, 2 * half)
        units = [unit_of(r2[i, b, :, lane(tiles)]) for b in range(nz - 1)]
        for j in range(tiles):
            acc = part[i, last, lane(j)]
            for b in range(nz - 1):
                acc = acc + widen(r2[i, b, :, lane(j)]) * units[b]
            acc = acc * (1.0 / total)
            cols = slice(i * width + j * LANES, i * width + (j + 1) * LANES)
            act_ref[:, cols] = acc[:BLK]
            gout_ref[:, cols] = acc[BLK:]

    for t in range(items + LAG_OUT):
        if t < items:
            local_terms(t)
        if 0 <= t - LAG_Y < items:
            chip_terms(t - LAG_Y)
        if 0 <= t - LAG_Z < items:
            pair_terms(t - LAG_Z)
        if 0 <= t - LAG_OUT < items:
            outputs(t - LAG_OUT)

    for i in range(items):
        core_copy[i].wait_send()
        y_copy[i].wait_send()
        for c in z_copy[i]:
            c.wait_send()


def on_device(n, tokens, out_grads, expert_ids):
    tok_rows, features = tokens.shape
    width = WIDTH if features % WIDTH == 0 else LANES
    items = features // width
    nz = n // 2
    half = n * PAIR
    coded = width + LANES
    total = tok_rows * n * 2
    vmem = pl.BlockSpec(memory_space=pltpu.VMEM)
    hbm = pl.BlockSpec(memory_space=pl.ANY)
    out = jax.ShapeDtypeStruct((BLK, features), jnp.float32)
    dma = pltpu.SemaphoreType.DMA
    flops = 2 * 3 * tok_rows * 2 * n * BLK * features
    act, grad = pl.pallas_call(
        functools.partial(kernel, n, width, total),
        out_shape=(out, out),
        in_specs=[vmem, hbm, hbm],
        out_specs=(vmem, vmem),
        scratch_shapes=[
            pltpu.VMEM((items, tok_rows, width), jnp.bfloat16),
            pltpu.VMEM((items, 2 * tok_rows, width), jnp.bfloat16),
            pltpu.VMEM((items, 2 * half, width), jnp.float32),
            pltpu.VMEM((items, half, width), jnp.float32),
            pltpu.VMEM((items, half // 2, coded), jnp.int16),
            pltpu.VMEM((items, half // 2, coded), jnp.int16),
            pltpu.VMEM((items, nz - 1, PAIR, coded), jnp.int16),
            pltpu.VMEM((items, nz - 1, PAIR, coded), jnp.int16),
            dma((2, items)),
            dma((items,)),
            dma((items,)),
            dma((items,)),
            dma((items,)),
            dma((items, nz - 1)),
            dma((items, nz - 1)),
        ],
        compiler_params=pltpu.CompilerParams(
            collective_id=0, has_side_effects=True, vmem_limit_bytes=61 * 1024 * 1024
        ),
        cost_estimate=pl.CostEstimate(
            flops=flops, bytes_accessed=6 * tok_rows * features + 8 * BLK * features,
            transcendentals=0,
        ),
    )(expert_ids.T, tokens, out_grads)
    shape = (ROWS_DEV, EXP_DEV, features)
    return act.reshape(shape), grad.reshape(shape)


def solution(mesh):
    placed = (
        P(("groups", "dp", "expert"), None),
        P(("groups", "dp", "expert"), None, None),
        P(("groups", "dp", "expert"), None),
    )
    return jax.shard_map(
        functools.partial(on_device, mesh.shape["dp"]),
        mesh=mesh,
        in_specs=placed,
        out_specs=(P(("groups", "dp"), "expert", None), P(("groups", "dp"), "expert", None)),
        check_vma=False,
    )
```

```python
import functools

import jax
import jax.numpy as jnp
from jax import lax
from jax.experimental import pallas as pl
from jax.experimental.pallas import tpu as pltpu
from jax.sharding import PartitionSpec as P

EXP_DEV = 2
ROWS_DEV = 4
BLK = EXP_DEV * ROWS_DEV
PAIR = 2 * BLK
LANES = 128
WIDTHS = (512, 1024, 1024, 1024, 1024, 1024, 512)
STEPS = 8.0
FULL = 32760.0
TINY = 1e-37
LAG_Y, LAG_Z, LAG_OUT = 1, 3, 4


def step_of(top):
    return jnp.ceil(jnp.log2(jnp.maximum(top, TINY)) * STEPS)


def scale_of(step):
    return jnp.exp2(step * (-1.0 / STEPS)) * FULL


def narrow(x):
    return jnp.round(x).astype(jnp.int32).astype(jnp.int16)


def widen(x):
    return x.astype(jnp.int32).astype(jnp.float32)


def unit_of(codes):
    return jnp.exp2(widen(codes) * (1.0 / STEPS)) * (1.0 / FULL)


def top_of(tiles):
    return functools.reduce(jnp.maximum, [jnp.abs(t) for t in tiles])


def widths_of(features):
    return WIDTHS if sum(WIDTHS) == features else (LANES,) * (features // LANES)


def starts_of(sizes):
    return [sum(sizes[:i]) for i in range(len(sizes))]


def kernel(
    n, total,
    ids_ref, tok_ref, grad_ref, act_ref, gout_ref,
    x_buf, g_buf, part, r0, s1, r1, s2, r2,
    in_sem, s0_sem, r0_sem, s1_sem, r1_sem, s2_sem, r2_sem,
):
    tok_rows, features = tok_ref.shape
    widths = widths_of(features)
    items = len(widths)
    begin = starts_of(widths)
    tiles = [w // LANES for w in widths]
    nz = n // 2
    half = n * PAIR
    quarter = half // 2
    blocks = quarter // PAIR
    marks = -(-2 * blocks // PAIR)
    y_tiles = [blocks * t + marks for t in tiles]
    y_at = starts_of(y_tiles)
    z_tiles = [t + 1 for t in tiles]
    z_at = starts_of(z_tiles)
    cols = [pl.ds(b, w) for b, w in zip(begin, widths)]
    core = lax.axis_index("expert")
    d = lax.axis_index("dp")
    z, y = d // 2, lax.rem(d, 2)

    flat = grad_ref.reshape(2 * tok_rows, features)
    loads = []
    for i in range(items):
        at = (slice(None), cols[i])
        pair = (
            pltpu.make_async_copy(tok_ref.at[at], x_buf.at[at], in_sem.at[0, i]),
            pltpu.make_async_copy(flat.at[at], g_buf.at[at], in_sem.at[1, i]),
        )
        loads.append(pair)
    for c in loads[0]:
        c.start()

    sibling = {"expert": 1 - core}
    across = {"dp": z * 2 + 1 - y}
    peers = [{"dp": lax.rem(z + 1 + j, nz) * 2 + y} for j in range(nz - 1)]
    barrier = pltpu.get_barrier_semaphore()
    for dev in [sibling, across] + peers:
        pl.semaphore_signal(barrier, inc=1, device_id=dev, device_id_type=pl.DeviceIdType.MESH)

    m_rows = 2 * n * BLK
    slab = -(-ROWS_DEV * n // LANES) * LANES

    def row_of(m):
        zd = z + 1 + (m & (n * BLK // 2 - 1)) // BLK
        zd = jnp.where(zd >= nz, zd - nz, zd)
        yd = (y + 1 + (m & (n * BLK - 1)) // (n * BLK // 2)) & 1
        return ROWS_DEV * (2 * zd + yd) + (m & (BLK - 1)) // EXP_DEV

    def expert_of(m):
        return EXP_DEV * ((core + 1 + m // (n * BLK)) & 1) + (m & (EXP_DEV - 1))

    pick = (
        row_of(lax.broadcasted_iota(jnp.int32, (m_rows, slab), 0))
        == lax.broadcasted_iota(jnp.int32, (m_rows, slab), 1)
    ).astype(jnp.float32).astype(jnp.bfloat16)
    ids = ids_ref[...]
    spread = (
        lax.broadcasted_iota(jnp.int32, (tok_rows, 2 * tok_rows), 1) // 2
        == lax.broadcasted_iota(jnp.int32, (tok_rows, 2 * tok_rows), 0)
    ).astype(jnp.float32).astype(jnp.bfloat16)
    ids_f = ids.astype(jnp.float32)
    both = jnp.dot(ids_f.astype(jnp.bfloat16), spread, preferred_element_type=jnp.float32)
    odd = (lax.broadcasted_iota(jnp.int32, (1, 2 * tok_rows), 1) & 1) == 1
    ids_flat = jnp.where(odd, both[1:2, :], both[0:1, :])
    e_tok = expert_of(lax.broadcasted_iota(jnp.int32, (m_rows, tok_rows), 0)).astype(jnp.float32)
    e_pair = expert_of(lax.broadcasted_iota(jnp.int32, (m_rows, 2 * tok_rows), 0)).astype(
        jnp.float32
    )
    nt = (((1,), (1,)), ((), ()))

    for c in loads[0]:
        c.wait()
    for pair in loads[1:]:
        for c in pair:
            c.start()
    left_x = lax.dot_general(pick, x_buf[:, :slab], nt, preferred_element_type=jnp.float32)
    left_g = lax.dot_general(pick, g_buf[:, :slab], nt, preferred_element_type=jnp.float32)
    hit_x = (e_tok == ids_f[0:1, :]) | (e_tok == ids_f[1:2, :])
    left_x = jnp.where(hit_x, left_x, 0.0).astype(jnp.bfloat16)
    left_g = jnp.where(e_pair == ids_flat, left_g, 0.0).astype(jnp.bfloat16)

    def send(src, dst, s_sem, r_sem, dev):
        return pltpu.make_async_remote_copy(
            src_ref=src, dst_ref=dst, send_sem=s_sem, recv_sem=r_sem,
            device_id=dev, device_id_type=pl.DeviceIdType.MESH,
        )

    core_copy = [
        send(
            part.at[pl.ds(0, half), cols[i]], r0.at[:, cols[i]],
            s0_sem.at[i], r0_sem.at[i], sibling,
        )
        for i in range(items)
    ]
    y_copy = []
    z_copy = []
    for i in range(items):
        run = pl.ds(y_at[i], y_tiles[i])
        y_copy.append(send(s1.at[run], r1.at[run], s1_sem.at[i], r1_sem.at[i], across))
        run = pl.ds(z_at[i], z_tiles[i])
        z_copy.append([
            send(
                s2.at[j, run], r2.at[j, run], s2_sem.at[i, j], r2_sem.at[i, j], peers[j]
            )
            for j in range(nz - 1)
        ])

    def local_terms(i):
        for a, (left, buf) in enumerate(((left_x, x_buf), (left_g, g_buf))):
            term = jnp.dot(left, buf[:, cols[i]], preferred_element_type=jnp.float32)
            for b in range(m_rows // BLK):
                part[b * PAIR + a * BLK : b * PAIR + (a + 1) * BLK, cols[i]] = term[
                    b * BLK : (b + 1) * BLK
                ]

    def lane(i, j):
        return slice(begin[i] + j * LANES, begin[i] + (j + 1) * LANES)

    def chip_terms(i):
        core_copy[i].wait_recv()
        steps = []
        for b in range(blocks):
            rows = slice(b * PAIR, (b + 1) * PAIR)
            own = slice(half + b * PAIR, half + (b + 1) * PAIR)
            sums = [part[own, lane(i, j)] + r0[rows, lane(i, j)] for j in range(tiles[i])]
            top = top_of(sums)
            scales = []
            for h in range(2):
                step = step_of(jnp.max(top[h * BLK : (h + 1) * BLK], axis=0, keepdims=True))
                steps.append(step)
                scales.append(jnp.broadcast_to(scale_of(step), (BLK, LANES)))
            scale = jnp.concatenate(scales, axis=0)
            for j, v in enumerate(sums):
                s1[y_at[i] + b * tiles[i] + j] = narrow(v * scale)
        steps += [jnp.zeros((1, LANES), jnp.float32)] * (marks * PAIR - len(steps))
        for m in range(marks):
            mark = jnp.concatenate(steps[m * PAIR : (m + 1) * PAIR], axis=0)
            s1[y_at[i] + blocks * tiles[i] + m] = narrow(mark)
        y_copy[i].start()

    def pair_terms(i):
        y_copy[i].wait_recv()
        units = [unit_of(r1[y_at[i] + blocks * tiles[i] + m]) for m in range(marks)]
        for b in range(blocks):
            near = slice(quarter + b * PAIR, quarter + (b + 1) * PAIR)
            own = slice(half + quarter + b * PAIR, half + quarter + (b + 1) * PAIR)
            unit = jnp.concatenate(
                [
                    jnp.broadcast_to(units[k // PAIR][k % PAIR : k % PAIR + 1], (BLK, LANES))
                    for k in (2 * b, 2 * b + 1)
                ],
                axis=0,
            )
            sums = [
                part[own, lane(i, j)]
                + r0[near, lane(i, j)]
                + widen(r1[y_at[i] + b * tiles[i] + j]) * unit
                for j in range(tiles[i])
            ]
            if b < blocks - 1:
                step = step_of(top_of(sums))
                scale = scale_of(step)
                for j, v in enumerate(sums):
                    s2[b, z_at[i] + j] = narrow(v * scale)
                s2[b, z_at[i] + tiles[i]] = narrow(step)
                z_copy[i][b].start()
            else:
                for j in range(tiles[i]):
                    part[own, lane(i, j)] = sums[j]

    def outputs(i):
        for c in z_copy[i]:
            c.wait_recv()
        last = slice(2 * half - PAIR, 2 * half)
        units = [unit_of(r2[b, z_at[i] + tiles[i]]) for b in range(nz - 1)]
        for j in range(tiles[i]):
            acc = part[last, lane(i, j)]
            for b in range(nz - 1):
                acc = acc + widen(r2[b, z_at[i] + j]) * units[b]
            acc = acc * (1.0 / total)
            act_ref[:, :, lane(i, j)] = acc[:BLK].reshape(ROWS_DEV, EXP_DEV, LANES)
            gout_ref[:, :, lane(i, j)] = acc[BLK:].reshape(ROWS_DEV, EXP_DEV, LANES)

    for t in range(items + LAG_OUT):
        if t < items:
            if t:
                for c in loads[t]:
                    c.wait()
            local_terms(t)
            if t == 0:
                pl.semaphore_wait(barrier, nz + 1)
            core_copy[t].start()
        if 0 <= t - LAG_Y < items:
            chip_terms(t - LAG_Y)
        if 0 <= t - LAG_Z < items:
            pair_terms(t - LAG_Z)
        if 0 <= t - LAG_OUT < items:
            outputs(t - LAG_OUT)

    for i in range(items):
        core_copy[i].wait_send()
        y_copy[i].wait_send()
        for c in z_copy[i]:
            c.wait_send()


def hand_over(act_ref, grad_ref, act_out, grad_out):
    act_out[...] = act_ref[...]
    grad_out[...] = grad_ref[...]


def on_device(n, tokens, out_grads, expert_ids):
    tok_rows, features = tokens.shape
    widths = widths_of(features)
    items = len(widths)
    nz = n // 2
    half = n * PAIR
    blocks = half // 2 // PAIR
    marks = -(-2 * blocks // PAIR)
    tiles = features // LANES
    y_shape = (blocks * tiles + marks * items, PAIR, LANES)
    z_shape = (nz - 1, tiles + items, PAIR, LANES)
    total = tok_rows * n * 2
    vmem = pl.BlockSpec(memory_space=pltpu.VMEM)
    hbm = pl.BlockSpec(memory_space=pl.ANY)
    out = jax.ShapeDtypeStruct((ROWS_DEV, EXP_DEV, features), jnp.float32)
    dma = pltpu.SemaphoreType.DMA
    flops = 2 * 3 * tok_rows * 2 * n * BLK * features
    act, grad = pl.pallas_call(
        functools.partial(kernel, n, total),
        out_shape=(out, out),
        in_specs=[vmem, hbm, hbm],
        out_specs=(vmem, vmem),
        scratch_shapes=[
            pltpu.VMEM((tok_rows, features), jnp.bfloat16),
            pltpu.VMEM((2 * tok_rows, features), jnp.bfloat16),
            pltpu.VMEM((2 * half, features), jnp.float32),
            pltpu.VMEM((half, features), jnp.float32),
            pltpu.VMEM(y_shape, jnp.int16),
            pltpu.VMEM(y_shape, jnp.int16),
            pltpu.VMEM(z_shape, jnp.int16),
            pltpu.VMEM(z_shape, jnp.int16),
            dma((2, items)),
            dma((items,)),
            dma((items,)),
            dma((items,)),
            dma((items,)),
            dma((items, nz - 1)),
            dma((items, nz - 1)),
        ],
        compiler_params=pltpu.CompilerParams(
            collective_id=0, has_side_effects=True, vmem_limit_bytes=61 * 1024 * 1024
        ),
        cost_estimate=pl.CostEstimate(
            flops=flops, bytes_accessed=6 * tok_rows * features + 8 * BLK * features,
            transcendentals=0,
        ),
    )(expert_ids.T, tokens, out_grads)
    return pl.pallas_call(
        hand_over,
        out_shape=(out, out),
        in_specs=[vmem, vmem],
        out_specs=(vmem, vmem),
    )(act, grad)


def solution(mesh):
    placed = (
        P(("groups", "dp", "expert"), None),
        P(("groups", "dp", "expert"), None, None),
        P(("groups", "dp", "expert"), None),
    )
    return jax.shard_map(
        functools.partial(on_device, mesh.shape["dp"]),
        mesh=mesh,
        in_specs=placed,
        out_specs=(P(("groups", "dp"), "expert", None), P(("groups", "dp"), "expert", None)),
        check_vma=False,
    )
```

```python
import functools

import jax
import jax.numpy as jnp
from jax import lax
from jax.experimental import pallas as pl
from jax.experimental.pallas import tpu as pltpu
from jax.sharding import PartitionSpec as P

EXP_DEV = 2
ROWS_DEV = 4
BLK = EXP_DEV * ROWS_DEV
PAIR = 2 * BLK
LANES = 128
WIDTHS = (1024, 1024, 1024, 1024, 1024, 1024)
STEPS = 8.0
FULL = 32760.0
TINY = 1e-37
LAG_Y, LAG_Z, LAG_OUT = 1, 2, 4


def step_of(top):
    return jnp.ceil(jnp.log2(jnp.maximum(top, TINY)) * STEPS)


def scale_of(step):
    return jnp.exp2(step * (-1.0 / STEPS)) * FULL


def narrow(x):
    return jnp.round(x).astype(jnp.int32).astype(jnp.int16)


def widen(x):
    return x.astype(jnp.int32).astype(jnp.float32)


def unit_of(codes):
    return jnp.exp2(widen(codes) * (1.0 / STEPS)) * (1.0 / FULL)


def top_of(tiles):
    return functools.reduce(jnp.maximum, [jnp.abs(t) for t in tiles])


def widths_of(features):
    return WIDTHS if sum(WIDTHS) == features else (LANES,) * (features // LANES)


def starts_of(sizes):
    return [sum(sizes[:i]) for i in range(len(sizes))]


def kernel(
    n, total,
    ids_ref, tok_ref, grad_ref, act_ref, gout_ref,
    x_buf, g_buf, part, r0, s1, r1, s2, r2,
    in_sem, s0_sem, r0_sem, s1_sem, r1_sem, s2_sem, r2_sem,
):
    tok_rows, features = tok_ref.shape
    widths = widths_of(features)
    items = len(widths)
    begin = starts_of(widths)
    tiles = [w // LANES for w in widths]
    nz = n // 2
    half = n * PAIR
    quarter = half // 2
    blocks = quarter // PAIR
    marks = -(-2 * blocks // PAIR)
    y_tiles = [blocks * t + marks for t in tiles]
    y_at = starts_of(y_tiles)
    z_tiles = [t + 1 for t in tiles]
    z_at = starts_of(z_tiles)
    cols = [pl.ds(b, w) for b, w in zip(begin, widths)]
    core = lax.axis_index("expert")
    d = lax.axis_index("dp")
    z, y = d // 2, lax.rem(d, 2)

    flat = grad_ref.reshape(2 * tok_rows, features)
    loads = []
    for i in range(items):
        at = (slice(None), cols[i])
        pair = (
            pltpu.make_async_copy(tok_ref.at[at], x_buf.at[at], in_sem.at[0, i]),
            pltpu.make_async_copy(flat.at[at], g_buf.at[at], in_sem.at[1, i]),
        )
        loads.append(pair)
    for c in loads[0]:
        c.start()

    sibling = {"expert": 1 - core}
    across = {"dp": z * 2 + 1 - y}
    peers = [{"dp": lax.rem(z + 1 + j, nz) * 2 + y} for j in range(nz - 1)]
    barrier = pltpu.get_barrier_semaphore()
    for dev in [sibling, across] + peers:
        pl.semaphore_signal(barrier, inc=1, device_id=dev, device_id_type=pl.DeviceIdType.MESH)

    m_rows = 2 * n * BLK
    slab = -(-ROWS_DEV * n // LANES) * LANES

    def row_of(m):
        zd = z + 1 + (m & (n * BLK // 2 - 1)) // BLK
        zd = jnp.where(zd >= nz, zd - nz, zd)
        yd = (y + 1 + (m & (n * BLK - 1)) // (n * BLK // 2)) & 1
        return ROWS_DEV * (2 * zd + yd) + (m & (BLK - 1)) // EXP_DEV

    def expert_of(m):
        return EXP_DEV * ((core + 1 + m // (n * BLK)) & 1) + (m & (EXP_DEV - 1))

    pick = (
        row_of(lax.broadcasted_iota(jnp.int32, (m_rows, slab), 0))
        == lax.broadcasted_iota(jnp.int32, (m_rows, slab), 1)
    ).astype(jnp.float32).astype(jnp.bfloat16)
    ids = ids_ref[...]
    spread = (
        lax.broadcasted_iota(jnp.int32, (tok_rows, 2 * tok_rows), 1) // 2
        == lax.broadcasted_iota(jnp.int32, (tok_rows, 2 * tok_rows), 0)
    ).astype(jnp.float32).astype(jnp.bfloat16)
    ids_f = ids.astype(jnp.float32)
    both = jnp.dot(ids_f.astype(jnp.bfloat16), spread, preferred_element_type=jnp.float32)
    odd = (lax.broadcasted_iota(jnp.int32, (1, 2 * tok_rows), 1) & 1) == 1
    ids_flat = jnp.where(odd, both[1:2, :], both[0:1, :])
    e_tok = expert_of(lax.broadcasted_iota(jnp.int32, (m_rows, tok_rows), 0)).astype(jnp.float32)
    e_pair = expert_of(lax.broadcasted_iota(jnp.int32, (m_rows, 2 * tok_rows), 0)).astype(
        jnp.float32
    )
    nt = (((1,), (1,)), ((), ()))

    for c in loads[0]:
        c.wait()
    for pair in loads[1:]:
        for c in pair:
            c.start()
    left_x = lax.dot_general(pick, x_buf[:, :slab], nt, preferred_element_type=jnp.float32)
    left_g = lax.dot_general(pick, g_buf[:, :slab], nt, preferred_element_type=jnp.float32)
    hit_x = (e_tok == ids_f[0:1, :]) | (e_tok == ids_f[1:2, :])
    left_x = jnp.where(hit_x, left_x, 0.0).astype(jnp.bfloat16)
    left_g = jnp.where(e_pair == ids_flat, left_g, 0.0).astype(jnp.bfloat16)

    def send(src, dst, s_sem, r_sem, dev):
        return pltpu.make_async_remote_copy(
            src_ref=src, dst_ref=dst, send_sem=s_sem, recv_sem=r_sem,
            device_id=dev, device_id_type=pl.DeviceIdType.MESH,
        )

    core_copy = [
        send(
            part.at[pl.ds(0, half), cols[i]], r0.at[:, cols[i]],
            s0_sem.at[i], r0_sem.at[i], sibling,
        )
        for i in range(items)
    ]
    y_copy = []
    z_copy = []
    for i in range(items):
        run = pl.ds(y_at[i], y_tiles[i])
        y_copy.append(send(s1.at[run], r1.at[run], s1_sem.at[i], r1_sem.at[i], across))
        run = pl.ds(z_at[i], z_tiles[i])
        z_copy.append([
            send(
                s2.at[j, run], r2.at[j, run], s2_sem.at[i, j], r2_sem.at[i, j], peers[j]
            )
            for j in range(nz - 1)
        ])

    def local_terms(i):
        for a, (left, buf) in enumerate(((left_x, x_buf), (left_g, g_buf))):
            term = jnp.dot(left, buf[:, cols[i]], preferred_element_type=jnp.float32)
            for b in range(m_rows // BLK):
                part[b * PAIR + a * BLK : b * PAIR + (a + 1) * BLK, cols[i]] = term[
                    b * BLK : (b + 1) * BLK
                ]

    def lane(i, j):
        return slice(begin[i] + j * LANES, begin[i] + (j + 1) * LANES)

    def chip_terms(i):
        core_copy[i].wait_recv()
        steps = []
        for b in range(blocks):
            rows = slice(b * PAIR, (b + 1) * PAIR)
            own = slice(half + b * PAIR, half + (b + 1) * PAIR)
            sums = [part[own, lane(i, j)] + r0[rows, lane(i, j)] for j in range(tiles[i])]
            top = top_of(sums)
            scales = []
            for h in range(2):
                step = step_of(jnp.max(top[h * BLK : (h + 1) * BLK], axis=0, keepdims=True))
                steps.append(step)
                scales.append(jnp.broadcast_to(scale_of(step), (BLK, LANES)))
            scale = jnp.concatenate(scales, axis=0)
            for j, v in enumerate(sums):
                s1[y_at[i] + b * tiles[i] + j] = narrow(v * scale)
        steps += [jnp.zeros((1, LANES), jnp.float32)] * (marks * PAIR - len(steps))
        for m in range(marks):
            mark = jnp.concatenate(steps[m * PAIR : (m + 1) * PAIR], axis=0)
            s1[y_at[i] + blocks * tiles[i] + m] = narrow(mark)
        y_copy[i].start()

    def pair_terms(i):
        y_copy[i].wait_recv()
        units = [unit_of(r1[y_at[i] + blocks * tiles[i] + m]) for m in range(marks)]
        for b in range(blocks):
            near = slice(quarter + b * PAIR, quarter + (b + 1) * PAIR)
            own = slice(half + quarter + b * PAIR, half + quarter + (b + 1) * PAIR)
            unit = jnp.concatenate(
                [
                    jnp.broadcast_to(units[k // PAIR][k % PAIR : k % PAIR + 1], (BLK, LANES))
                    for k in (2 * b, 2 * b + 1)
                ],
                axis=0,
            )
            sums = [
                part[own, lane(i, j)]
                + r0[near, lane(i, j)]
                + widen(r1[y_at[i] + b * tiles[i] + j]) * unit
                for j in range(tiles[i])
            ]
            if b < blocks - 1:
                step = step_of(top_of(sums))
                scale = scale_of(step)
                for j, v in enumerate(sums):
                    s2[b, z_at[i] + j] = narrow(v * scale)
                s2[b, z_at[i] + tiles[i]] = narrow(step)
                z_copy[i][b].start()
            else:
                for j in range(tiles[i]):
                    part[own, lane(i, j)] = sums[j]

    def outputs(i):
        for c in z_copy[i]:
            c.wait_recv()
        last = slice(2 * half - PAIR, 2 * half)
        units = [unit_of(r2[b, z_at[i] + tiles[i]]) for b in range(nz - 1)]
        for j in range(tiles[i]):
            acc = part[last, lane(i, j)]
            for b in range(nz - 1):
                acc = acc + widen(r2[b, z_at[i] + j]) * units[b]
            acc = acc * (1.0 / total)
            act_ref[:, :, lane(i, j)] = acc[:BLK].reshape(ROWS_DEV, EXP_DEV, LANES)
            gout_ref[:, :, lane(i, j)] = acc[BLK:].reshape(ROWS_DEV, EXP_DEV, LANES)

    for t in range(items + LAG_OUT):
        if t < items:
            if t:
                for c in loads[t]:
                    c.wait()
            local_terms(t)
            if t == 0:
                pl.semaphore_wait(barrier, nz + 1)
            core_copy[t].start()
        if 0 <= t - LAG_Y < items:
            chip_terms(t - LAG_Y)
        if 0 <= t - LAG_Z < items:
            pair_terms(t - LAG_Z)
        if 0 <= t - LAG_OUT < items:
            outputs(t - LAG_OUT)

    for i in range(items):
        core_copy[i].wait_send()
        y_copy[i].wait_send()
        for c in z_copy[i]:
            c.wait_send()


def hand_over(act_ref, grad_ref, act_out, grad_out):
    act_out[...] = act_ref[...]
    grad_out[...] = grad_ref[...]


def on_device(n, tokens, out_grads, expert_ids):
    tok_rows, features = tokens.shape
    widths = widths_of(features)
    items = len(widths)
    nz = n // 2
    half = n * PAIR
    blocks = half // 2 // PAIR
    marks = -(-2 * blocks // PAIR)
    tiles = features // LANES
    y_shape = (blocks * tiles + marks * items, PAIR, LANES)
    z_shape = (nz - 1, tiles + items, PAIR, LANES)
    total = tok_rows * n * 2
    vmem = pl.BlockSpec(memory_space=pltpu.VMEM)
    hbm = pl.BlockSpec(memory_space=pl.ANY)
    out = jax.ShapeDtypeStruct((ROWS_DEV, EXP_DEV, features), jnp.float32)
    dma = pltpu.SemaphoreType.DMA
    flops = 2 * 3 * tok_rows * 2 * n * BLK * features
    act, grad = pl.pallas_call(
        functools.partial(kernel, n, total),
        out_shape=(out, out),
        in_specs=[vmem, hbm, hbm],
        out_specs=(vmem, vmem),
        scratch_shapes=[
            pltpu.VMEM((tok_rows, features), jnp.bfloat16),
            pltpu.VMEM((2 * tok_rows, features), jnp.bfloat16),
            pltpu.VMEM((2 * half, features), jnp.float32),
            pltpu.VMEM((half, features), jnp.float32),
            pltpu.VMEM(y_shape, jnp.int16),
            pltpu.VMEM(y_shape, jnp.int16),
            pltpu.VMEM(z_shape, jnp.int16),
            pltpu.VMEM(z_shape, jnp.int16),
            dma((2, items)),
            dma((items,)),
            dma((items,)),
            dma((items,)),
            dma((items,)),
            dma((items, nz - 1)),
            dma((items, nz - 1)),
        ],
        compiler_params=pltpu.CompilerParams(
            collective_id=0, has_side_effects=True, vmem_limit_bytes=61 * 1024 * 1024
        ),
        cost_estimate=pl.CostEstimate(
            flops=flops, bytes_accessed=6 * tok_rows * features + 8 * BLK * features,
            transcendentals=0,
        ),
    )(expert_ids.T, tokens, out_grads)
    return pl.pallas_call(
        hand_over,
        out_shape=(out, out),
        in_specs=[vmem, vmem],
        out_specs=(vmem, vmem),
    )(act, grad)


def solution(mesh):
    placed = (
        P(("groups", "dp", "expert"), None),
        P(("groups", "dp", "expert"), None, None),
        P(("groups", "dp", "expert"), None),
    )
    return jax.shard_map(
        functools.partial(on_device, mesh.shape["dp"]),
        mesh=mesh,
        in_specs=placed,
        out_specs=(P(("groups", "dp"), "expert", None), P(("groups", "dp"), "expert", None)),
        check_vma=False,
    )
```
